32 devices in a mesh: rep: 4 (over y, x), exp: 8 (over z, core).
Axes of the slice: x: 2, y: 2, z: 4, core: 2. Of those that a mesh axis runs over, the one named last changes fastest.
Arguments:
- tokens: bfloat16 [4, 1024, 2048], P('rep', 'exp'), may hold values from -6 to 6
- cotangent: bfloat16 [4, 1024, 2048], P('rep', 'exp'), may hold values from -12 to 12
- route_weight: float32 [4, 1024, 8], P('rep', 'exp'), may hold values from 0.05 to 0.25
- expert_ids: int32 [4, 1024, 8], P('rep', 'exp'), may hold values from 0 to 15, as said below
- slots: int32 [4, 1024, 8], P('rep', 'exp'), may hold values from 0 to 127, as said below
- gossip_round: int32 [1], replicated, may hold values from 0 to 127
- w_in: bfloat16 [4, 16, 2048, 768], P('rep', 'exp'), may hold values from -4 to 4
- w_out: bfloat16 [4, 16, 384, 2048], P('rep', 'exp'), may hold values from -4 to 4
- mom_in: bfloat16 [4, 16, 2048, 768], P('rep', 'exp'), may hold values from -3 to 3
- mom_out: bfloat16 [4, 16, 384, 2048], P('rep', 'exp'), may hold values from -3 to 3
Outputs:
- layer_out: bfloat16 [4, 1024, 2048], P('rep', 'exp')
- grad_tokens: bfloat16 [4, 1024, 2048], P('rep', 'exp')
- new_w_in: bfloat16 [4, 16, 2048, 768], P('rep', 'exp')
- new_w_out: bfloat16 [4, 16, 384, 2048], P('rep', 'exp')
- new_mom_in: bfloat16 [4, 16, 2048, 768], P('rep', 'exp')
- new_mom_out: bfloat16 [4, 16, 384, 2048], P('rep', 'exp')
The draws below stay inside these ranges and needn't reach their ends.
Inputs may be any that keep to these rules, and one draw needn't show every extreme that they name: `expert_ids`: each token names 8 different experts. `slots`: the slot of a choice is the number of earlier tokens of the same aligned block of 128 tokens of its replica that name the same expert; in every block some expert is named by all tokens. `gossip_round`: the peer of replica k is k xor 2^(t mod 2).
All inputs are finite; a program needn't handle non-finite values.
Results may differ from the reference program's by a relative error of at most 0.0052.
Values may be sent and summed in bfloat16 or wider, within the bound.
No kernel may reach another device: no remote copies, remote signals or barrier semaphores. Data moves between devices by JAX's collectives and lax.ppermute only.
A program may use at most 128 MiB of HBM per device.

```python
import math
import jax
import jax.numpy as jnp
from jax import lax

D = 2048
FF = 384
SPECIALIST_COUNT = 16
TOP = 8
TOK_DEV = 128
CAP = 64
TOKENS = 1024
REPLICAS = 4
LOG_REP = 2
N_EXP = 8


def routing_table(key):
    key_pop, key_noise, key_hot = jax.random.split(key, 3)
    blocks = TOKENS // TOK_DEV
    crowded_specialist = jax.random.randint(key_pop, (REPLICAS, 1, SPECIALIST_COUNT), 0, 16) * 128
    gating_noise = jax.random.randint(key_noise, (REPLICAS, TOKENS, SPECIALIST_COUNT), 0, 4096)
    hot_block = jax.random.randint(key_hot, (REPLICAS, blocks, 1), 0, SPECIALIST_COUNT)
    preferred_item = jnp.repeat(hot_block, TOK_DEV, axis=1)
    field_positions = jnp.arange(SPECIALIST_COUNT, dtype=jnp.int32)
    extra_preference = jnp.where(field_positions[None, None, :] == preferred_item, 1 << 20, 0)
    gating_affinity = (gating_noise + crowded_specialist + extra_preference) * SPECIALIST_COUNT + field_positions[None, None, :]
    unused, chosen = lax.top_k(gating_affinity, TOP)
    chosen = chosen.astype(jnp.int32)
    member = jnp.any(chosen[:, :, :, None] == field_positions[None, None, None, :], axis=2).astype(jnp.int32)
    member = member.reshape(REPLICAS, blocks, TOK_DEV, SPECIALIST_COUNT)
    earlier = (jnp.cumsum(member, axis=2) - member).reshape(REPLICAS, TOKENS, SPECIALIST_COUNT)
    places = jnp.take_along_axis(earlier, chosen, axis=2).astype(jnp.int32)
    return (chosen, places)


def draw_expert_ids(key, part):
    chosen, places = routing_table(key)
    return chosen


def draw_slots(key, part):
    chosen, places = routing_table(key)
    return places


def block_scale(rng, shape, cuts, low, high):
    def one(axis_at, shards_of):
        steps = jax.random.uniform(jax.random.fold_in(jax.random.fold_in(rng, 6), axis_at), (shards_of,), jnp.float32, low / len(cuts), high / len(cuts))
        return jnp.repeat(jnp.exp(steps), shape[axis_at] // shards_of).reshape((-1,) + (1,) * (len(shape) - axis_at - 1))

    gain = one(*cuts[0])
    for cut in cuts[1:]:
        gain = gain * one(*cut)
    return gain


def normal_values(stream_key, shape, spread, bound, cuts=(), held_as=jnp.bfloat16):
    values = jax.random.normal(stream_key, shape, jnp.float32) * spread
    if len(cuts) > 0:
        values = block_scale(stream_key, shape, cuts, -0.22, 0.18) * values
    return jnp.clip(values, min=-bound, max=bound).astype(held_as)


def setup_inputs(seed: int = 0) -> dict:
    key_list = jax.random.split(jax.random.key(seed), 11)
    return {
        "tokens": normal_values(key_list[0], (REPLICAS, TOKENS, D), 1.0, 6.0, ((0, 4), (1, 8))),
        "cotangent": normal_values(key_list[1], (REPLICAS, TOKENS, D), 2.0, 12.0, ((0, 4), (1, 8))),
        "route_weight": jnp.clip(0.05 + 0.2 * jax.random.uniform(key_list[2], (REPLICAS, TOKENS, TOP), jnp.float32) ** block_scale(key_list[2], (REPLICAS, TOKENS, TOP), ((0, 4), (1, 8)), -0.2, 0.2), 0.05, 0.25),
        "expert_ids": draw_expert_ids(jax.random.fold_in(key_list[10], 71), 0),
        "slots": draw_slots(jax.random.fold_in(key_list[10], 71), 0),
        "gossip_round": jax.random.randint(key_list[5], (1,), 0, 64 * LOG_REP).astype(jnp.int32),
        "w_in": normal_values(key_list[6], (REPLICAS, SPECIALIST_COUNT, D, 2 * FF), 1.0, 4.0, ((0, 4), (1, 8))),
        "w_out": normal_values(key_list[7], (REPLICAS, SPECIALIST_COUNT, FF, D), 1.0, 4.0, ((0, 4), (1, 8))),
        "mom_in": normal_values(key_list[8], (REPLICAS, SPECIALIST_COUNT, D, 2 * FF), 0.5, 3.0, ((0, 4), (1, 8))),
        "mom_out": normal_values(key_list[9], (REPLICAS, SPECIALIST_COUNT, FF, D), 0.5, 3.0, ((0, 4), (1, 8))),
    }


MOMENTUM_DECAY = 0.9
STEP_SIZE = 0.2

def activation(gate):
    sigmoid = jax.nn.sigmoid(gate)
    return (gate * sigmoid, sigmoid * (1.0 + gate * (1.0 - sigmoid)))

def combine(base, rows, target, factor):
    flat = jnp.concatenate([rows.reshape(-1, D), jnp.zeros((1, D), jnp.bfloat16)])
    picked = flat[target].astype(jnp.float32)
    if factor is not None:
        picked = picked * factor[:, :, None]
    return (base.astype(jnp.float32) + lax.optimization_barrier(jnp.sum(picked, axis=1))).astype(jnp.bfloat16)

def replica_step(operands):
    inputs, upstream, weights, chosen, places, proj_in, proj_out, moment_in, moment_out = operands
    rows_per = N_EXP * CAP
    scale_in = 1.0 / math.sqrt(D)
    scale_out = 1.0 / math.sqrt(FF)
    block_of = (jnp.arange(TOKENS, dtype=jnp.int32) // TOK_DEV)[:, None]
    target = jnp.where(places < CAP, chosen * rows_per + block_of * CAP + places, SPECIALIST_COUNT * rows_per).astype(jnp.int32)
    numbered = jnp.arange(TOKENS * TOP, dtype=jnp.int32)
    table = jnp.full((SPECIALIST_COUNT * rows_per + 1,), TOKENS * TOP, jnp.int32).at[target.reshape(-1)].set(numbered)
    table = table[:SPECIALIST_COUNT * rows_per].reshape(SPECIALIST_COUNT, rows_per)
    padded_in = jnp.concatenate([inputs, jnp.zeros((1, D), jnp.bfloat16)])
    padded_up = jnp.concatenate([upstream, jnp.zeros((1, D), jnp.bfloat16)])
    padded_weight = jnp.concatenate([weights.reshape(-1), jnp.zeros((1,), jnp.float32)])

    def one_expert(parts):
        entries, weight_in, weight_out, momentum_in, momentum_out = parts
        source_row = entries // TOP
        rows_in = padded_in[source_row]
        grad_rows = (padded_weight[entries][:, None] * padded_up[source_row].astype(jnp.float32)).astype(jnp.bfloat16)
        joint = jnp.dot(rows_in, weight_in, preferred_element_type=jnp.float32) * scale_in
        gate = joint[:, :FF]
        upper = joint[:, FF:]
        act_value, act_slope = activation(gate)
        inner = (act_value * upper).astype(jnp.bfloat16)
        result = (jnp.dot(inner, weight_out, preferred_element_type=jnp.float32) * scale_out).astype(jnp.bfloat16)
        grad_inner = jnp.dot(grad_rows, weight_out.T, preferred_element_type=jnp.float32) * scale_out
        grad_out = jnp.dot(inner.T, grad_rows, preferred_element_type=jnp.float32) * scale_out
        grad_joint = jnp.concatenate([grad_inner * upper * act_slope, grad_inner * act_value], axis=1).astype(jnp.bfloat16)
        grad_in = jnp.dot(rows_in.T, grad_joint, preferred_element_type=jnp.float32) * scale_in
        grad_rows_in = (jnp.dot(grad_joint, weight_in.T, preferred_element_type=jnp.float32) * scale_in).astype(jnp.bfloat16)
        new_moment_in = MOMENTUM_DECAY * momentum_in.astype(jnp.float32) + grad_in
        new_moment_out = MOMENTUM_DECAY * momentum_out.astype(jnp.float32) + grad_out
        update_in = (weight_in.astype(jnp.float32) - STEP_SIZE * new_moment_in).astype(jnp.bfloat16)
        update_out = (weight_out.astype(jnp.float32) - STEP_SIZE * new_moment_out).astype(jnp.bfloat16)
        return (result, grad_rows_in, update_in, update_out, new_moment_in.astype(jnp.bfloat16), new_moment_out.astype(jnp.bfloat16))
    result, grad_rows_in, update_in, update_out, next_in, next_out = lax.map(one_expert, (table, proj_in, proj_out, moment_in, moment_out))
    layer_out = combine(inputs, result, target, weights)
    grad_tokens = combine(upstream, grad_rows_in, target, None)
    return (layer_out, grad_tokens, update_in, update_out, next_in, next_out)

def reference(tokens, cotangent, route_weight, expert_ids, slots, gossip_round, w_in, w_out, mom_in, mom_out):
    layer_out, grad_tokens, update_in, update_out, next_in, next_out = lax.map(replica_step, (tokens, cotangent, route_weight, expert_ids, slots, w_in, w_out, mom_in, mom_out))
    round_now = jnp.remainder(gossip_round[0].astype(jnp.int32), jnp.int32(LOG_REP))
    peers = jnp.bitwise_xor(jnp.arange(REPLICAS, dtype=jnp.int32), jnp.left_shift(jnp.int32(1), round_now))
    new_w_in = (0.5 * (update_in.astype(jnp.float32) + update_in[peers].astype(jnp.float32))).astype(jnp.bfloat16)
    new_w_out = (0.5 * (update_out.astype(jnp.float32) + update_out[peers].astype(jnp.float32))).astype(jnp.bfloat16)
    return (layer_out, grad_tokens, new_w_in, new_w_out, next_in, next_out)
```

```python
from functools import partial
import math

import jax
import jax.numpy as jnp
from jax import lax
from jax.experimental import pallas as pl
from jax.experimental.pallas import tpu as pltpu
from jax.sharding import PartitionSpec as P

CAP = 64
MOMENTUM_DECAY = 0.9
STEP_SIZE = 0.2
COLS = 512
F32 = jnp.float32
BF16 = jnp.bfloat16
VMEM = 48 * 1024 * 1024


def place(index, hops, other):
    size = lax.axis_size("exp")
    return (index // 2 * 2 + 2 * hops + size) % size + (index % 2 + other) % 2


def shift(value, hops, other=0):
    size = lax.axis_size("exp")
    return lax.ppermute(value, "exp", [(i, place(i, hops, other)) for i in range(size)])


def swap(value):
    return shift(value, 0, 1)


def gossip(value, bit):
    size = lax.axis_size("rep")
    return lax.ppermute(value, "rep", [(i, i ^ (1 << bit)) for i in range(size)])


def after(value, *first):
    return lax.optimization_barrier((value, *first))[0]


def from_chips(value):
    chips = lax.axis_size("exp") // 2
    return [value] + [shift(value, s) for s in range(1, chips)]


def with_other_core(same):
    return [part for block in same for part in (block, swap(block))]


def nn(a, b):
    return jnp.dot(a, b, preferred_element_type=F32)


def nt(a, b):
    return lax.dot_general(a, b, (((1,), (1,)), ((), ())), preferred_element_type=F32)


def tn(a, b):
    return lax.dot_general(a, b, (((0,), (0,)), ((), ())), preferred_element_type=F32)


def kernel_call(body, grid, ins, outs, scratch=(), flops=0, aliases=None):
    def spec(block, where):
        if block is None:
            return pl.BlockSpec(memory_space=pl.ANY)
        return pl.BlockSpec(block, where)

    moved = sum(math.prod(a.shape) * a.dtype.itemsize for a, block, _ in list(ins) + list(outs) if block is not None)
    return pl.pallas_call(
        body,
        grid=grid,
        in_specs=[spec(b, w) for _, b, w in ins],
        out_specs=[spec(b, w) for _, b, w in outs],
        out_shape=[jax.ShapeDtypeStruct(a.shape, a.dtype) for a, _, _ in outs],
        scratch_shapes=list(scratch),
        input_output_aliases=aliases or {},
        compiler_params=pltpu.CompilerParams(vmem_limit_bytes=VMEM),
        cost_estimate=pl.CostEstimate(flops=flops // 1000, bytes_accessed=moved // 1000, transcendentals=0),
    )(*[a for a, _, _ in ins])


def shape(dims, dtype):
    return jax.ShapeDtypeStruct(dims, dtype)


def matches(mine_ref, k, local):
    tokens = mine_ref.shape[2]
    slot = lax.broadcasted_iota(jnp.int32, (CAP, tokens), 0).astype(F32)
    return [mine_ref[k, 2 * a : 2 * a + 1, :] == slot for a in range(local)]


def onehot(found):
    return jnp.concatenate([f.astype(F32) for f in found], axis=0).astype(BF16)


def row_weights(mine_ref, k, found):
    return [
        jnp.sum(jnp.where(f, mine_ref[k, 2 * a + 1 : 2 * a + 2, :], 0.0), axis=1, keepdims=True)
        for a, f in enumerate(found)
    ]


def fill_rows(blocks, mine_ref, rows_ref, local, weighted):
    for k, block in enumerate(blocks):
        found = matches(mine_ref, k, local)
        rows = nn(onehot(found), block[...])
        weight = row_weights(mine_ref, k, found) if weighted else None
        for a in range(local):
            part = rows[a * CAP : (a + 1) * CAP]
            if weighted:
                part = part * weight[a]
            rows_ref[a, k * CAP : (k + 1) * CAP, :] = part.astype(BF16)


def forward_body(groups, local, hidden, scale, *refs):
    blocks, (mine, w, rows, inner, slope, value, joint) = refs[:groups], refs[groups:]
    fill_rows(blocks, mine, rows, local, False)
    first = pl.program_id(0) == 0

    for a in range(local):
        part = nn(rows[a], w[a])

        @pl.when(first)
        def _():
            joint[a] = part

        @pl.when(jnp.logical_not(first))
        def _():
            joint[a] += part

    @pl.when(pl.program_id(0) == pl.num_programs(0) - 1)
    def _():
        for a in range(local):
            gate = joint[a, :, :hidden] * scale
            upper = joint[a, :, hidden:] * scale
            sigmoid = jax.nn.sigmoid(gate)
            act = gate * sigmoid
            inner[a] = (act * upper).astype(BF16)
            slope[a] = upper * (sigmoid * (1.0 + gate * (1.0 - sigmoid)))
            value[a] = act


def forward(blocks, mine, proj_in):
    groups = len(blocks)
    local, width, double = proj_in.shape
    hidden, rows, tokens = double // 2, groups * CAP, blocks[0].shape[0]
    whole = lambda j: (0, 0, 0)
    return kernel_call(
        partial(forward_body, groups, local, hidden, 1.0 / math.sqrt(width)),
        (width // COLS,),
        [(b, (tokens, COLS), lambda j: (0, j)) for b in blocks]
        + [(mine, mine.shape, whole), (proj_in, (local, COLS, double), lambda j: (0, j, 0))],
        [
            (shape((local, rows, width), BF16), (local, rows, COLS), lambda j: (0, 0, j)),
            (shape((local, rows, hidden), BF16), (local, rows, hidden), whole),
            (shape((local, rows, hidden), F32), (local, rows, hidden), whole),
            (shape((local, rows, hidden), F32), (local, rows, hidden), whole),
        ],
        [pltpu.VMEM((local, rows, double), F32)],
        2 * local * rows * width * double,
    )


def backward_body(groups, local, hidden, scale, *refs):
    blocks = refs[:groups]
    mine, inner, slope, value, w, mom, new_mom, update, grad_joint, rows, grad_inner = refs[groups:]
    fill_rows(blocks, mine, rows, local, True)
    first = pl.program_id(0) == 0

    for a in range(local):
        moment = MOMENTUM_DECAY * mom[a].astype(F32) + tn(inner[a], rows[a]) * scale
        new_mom[a] = moment.astype(BF16)
        update[a] = (w[a].astype(F32) - STEP_SIZE * moment).astype(BF16)
        part = nt(rows[a], w[a])

        @pl.when(first)
        def _():
            grad_inner[a] = part

        @pl.when(jnp.logical_not(first))
        def _():
            grad_inner[a] += part

    @pl.when(pl.program_id(0) == pl.num_programs(0) - 1)
    def _():
        for a in range(local):
            grad = grad_inner[a] * scale
            grad_joint[a, :, :hidden] = (grad * slope[a]).astype(BF16)
            grad_joint[a, :, hidden:] = (grad * value[a]).astype(BF16)


def backward(blocks, mine, inner, slope, value, proj_out, mom_out):
    groups = len(blocks)
    local, hidden, width = proj_out.shape
    rows, tokens = groups * CAP, blocks[0].shape[0]
    whole = lambda j: (0, 0, 0)
    cut = ((local, hidden, COLS), lambda j: (0, 0, j))
    held = ((local, rows, hidden), whole)
    return kernel_call(
        partial(backward_body, groups, local, hidden, 1.0 / math.sqrt(hidden)),
        (width // COLS,),
        [(b, (tokens, COLS), lambda j: (0, j)) for b in blocks]
        + [(mine, mine.shape, whole), (inner, *held), (slope, *held), (value, *held), (proj_out, *cut), (mom_out, *cut)],
        [
            (proj_out, *cut),
            (proj_out, *cut),
            (shape((local, rows, 2 * hidden), BF16), (local, rows, 2 * hidden), whole),
        ],
        [pltpu.VMEM((local, rows, COLS), BF16), pltpu.VMEM((local, rows, hidden), F32)],
        4 * local * rows * width * hidden,
    )


def peer_body(groups, local, scale, *refs):
    blocks, (mine, inner, base, update, new_w, rows) = refs[:groups], refs[groups:]
    fill_rows(blocks, mine, rows, local, True)
    for a in range(local):
        theirs = base[a].astype(F32) - STEP_SIZE * (tn(inner[a], rows[a]) * scale)
        new_w[a] = (0.5 * (update[a].astype(F32) + theirs)).astype(BF16)


def peer_out(blocks, mine, inner, base, update):
    groups = len(blocks)
    local, hidden, width = base.shape
    rows, tokens = groups * CAP, blocks[0].shape[0]
    whole = lambda j: (0, 0, 0)
    cut = ((local, hidden, COLS), lambda j: (0, 0, j))
    return kernel_call(
        partial(peer_body, groups, local, 1.0 / math.sqrt(hidden)),
        (width // COLS,),
        [(b, (tokens, COLS), lambda j: (0, j)) for b in blocks]
        + [(mine, mine.shape, whole), (inner, (local, rows, hidden), whole), (base, *cut), (update, *cut)],
        [(base, *cut)],
        [pltpu.VMEM((local, rows, COLS), BF16)],
        2 * local * rows * width * hidden,
    )[0]


def base_body(w, mom, base):
    base[...] = (w[...].astype(F32) - (STEP_SIZE * MOMENTUM_DECAY) * mom[...].astype(F32)).astype(BF16)


def base_out(proj_out, mom_out):
    local, hidden, width = proj_out.shape
    cut = ((1, hidden, width // 2), lambda a, j: (a, 0, j))
    return kernel_call(base_body, (local, 2), [(proj_out, *cut), (mom_out, *cut)], [(proj_out, *cut)])[0]


def grad_in_body(scale, rows, grad_joint, w, mom, *rest):
    update, new_mom = rest[-2:]
    moment = MOMENTUM_DECAY * mom[0].astype(F32) + tn(rows[0], grad_joint[0]) * scale
    new_mom[0] = moment.astype(BF16)
    update[0] = (w[0].astype(F32) - STEP_SIZE * moment).astype(BF16)


def grad_in(rows_in, grad_joint, proj_in, mom_in, index, depth, held):
    local, width, double = proj_in.shape
    rows = rows_in.shape[1]
    cut = ((1, depth, double), lambda a: (a, index, 0))
    ins = [
        (rows_in, (1, rows, depth), lambda a: (a, 0, index)),
        (grad_joint, (1, rows, double), lambda a: (a, 0, 0)),
        (proj_in, *cut),
        (mom_in, *cut),
    ]
    if held is not None:
        ins.append((held, None, None))
    return kernel_call(
        partial(grad_in_body, 1.0 / math.sqrt(width)),
        (local,),
        ins,
        [(shape((local, depth, double), BF16), (1, depth, double), lambda a: (a, 0, 0)), (proj_in, *cut)],
        flops=2 * local * rows * depth * double,
        aliases={4: 1} if held is not None else None,
    )


def average_body(own, peer, *rest):
    rest[-1][...] = (0.5 * (own[...].astype(F32) + peer[...].astype(F32))).astype(BF16)


def average(own, peer, like, index, held):
    local, depth, double = own.shape
    block = (1, depth, double)
    ins = [(own, block, lambda a: (a, 0, 0)), (peer, block, lambda a: (a, 0, 0))]
    if held is not None:
        ins.append((held, None, None))
    return kernel_call(
        average_body,
        (local,),
        ins,
        [(like, block, lambda a: (a, index, 0))],
        aliases={2: 0} if held is not None else None,
    )[0]


def returns_body(groups, local, scale, weighted, product, left, w, mine, own, other, rows):
    for a in range(local):
        rows[a] = (product(left[a], w[a]) * scale).astype(rows.dtype)
    for k in range(groups):
        found = matches(mine, k, local)
        weight = row_weights(mine, k, found) if weighted else None
        parts = [rows[a, k * CAP : (k + 1) * CAP, :] for a in range(local)]
        if weighted:
            parts = [p * weight[a] for a, p in enumerate(parts)]
        part = tn(onehot(found), jnp.concatenate([p.astype(BF16) for p in parts], axis=0))
        if k % 2 == 0:
            own[k // 2] = part
        else:
            other[k // 2] = part.astype(BF16)


def returns(left, w, mine, weighted):
    groups, _, tokens = mine.shape
    local, rows, inside = left.shape
    whole = lambda j: (0, 0, 0)
    if weighted:
        product, width, cut, scale = nn, w.shape[2], ((local, inside, COLS), lambda j: (0, 0, j)), 1.0 / math.sqrt(inside)
    else:
        product, width, cut, scale = nt, w.shape[1], ((local, COLS, inside), lambda j: (0, j, 0)), 1.0 / math.sqrt(w.shape[1])
    out = ((groups // 2, tokens, COLS), lambda j: (0, 0, j))
    return kernel_call(
        partial(returns_body, groups, local, scale, weighted, product),
        (width // COLS,),
        [(left, left.shape, whole), (w, *cut), (mine, mine.shape, whole)],
        [(shape((groups // 2, tokens, width), F32), *out), (shape((groups // 2, tokens, width), BF16), *out)],
        [pltpu.VMEM((local, rows, COLS), F32 if weighted else BF16)],
        2 * local * rows * width * inside,
    )


def routing(weights, chosen, places, local):
    groups = lax.axis_size("exp")
    tokens = chosen.shape[0]
    ids = jnp.arange(groups * local, dtype=jnp.int32)[:, None, None]
    hit = (chosen[None] == ids) & (places[None] < CAP)
    place_of = (jnp.sum(jnp.where(hit, places[None] + 1, 0), axis=2) - 1).astype(F32)
    weight_of = jnp.sum(jnp.where(hit, weights[None], 0.0), axis=2)
    packed = jnp.stack([place_of, weight_of], axis=1).reshape(groups, 2 * local, tokens)
    arrived = lax.all_to_all(packed, "exp", split_axis=0, concat_axis=0, tiled=True)
    here = lax.axis_index("exp")
    order = [place(here, -hops, other) for hops in range(groups // 2) for other in range(2)]
    return arrived[jnp.stack(order)]


def collect(base, own, other, first):
    pairs = own + swap(other).astype(F32)
    total = base.astype(F32) + pairs[0]
    short = after(pairs[1:].astype(BF16), *first)
    back = [shift(short[s], -s - 1) for s in range(short.shape[0])]
    for part in back:
        total = total + part.astype(F32)
    return total.astype(BF16), back


def step(inputs, upstream, weights, chosen, places, proj_in, proj_out, mom_in, mom_out, bit):
    local, width, _ = proj_in.shape
    depth = 512

    tokens_same = from_chips(inputs)
    mine = routing(weights, chosen, places, local)
    base = base_out(proj_out, mom_out)
    peer_upstream = gossip(upstream, bit)
    peer_base = gossip(base, bit)
    upstream_same = from_chips(after(upstream, *tokens_same))
    tokens_all = with_other_core(tokens_same)
    tokens_all[-1] = after(tokens_all[-1], base)
    rows_in, inner, slope, value = forward(tokens_all, mine, proj_in)

    peer_inner = gossip(inner, bit)
    peer_mine = gossip(after(mine, inner), bit)
    upstream_all = with_other_core(upstream_same)
    upstream_all[-1], peer_upstream, peer_base = lax.optimization_barrier((upstream_all[-1], peer_upstream, peer_base))
    new_mom_out, update_out, grad_joint = backward(upstream_all, mine, inner, slope, value, proj_out, mom_out)
    grad_joint, peer_inner, peer_mine = lax.optimization_barrier((grad_joint, peer_inner, peer_mine))
    peer_same = from_chips(after(peer_upstream, *upstream_same))

    updates, peers = [], []
    new_mom_in = new_w_in = None

    def next_chunk(new_mom_in, *first):
        i = len(updates)
        update, new_mom_in = grad_in(rows_in, after(grad_joint, *first), proj_in, mom_in, i, depth, new_mom_in)
        updates.append(update)
        peers.append(gossip(update, bit))
        return new_mom_in

    new_mom_in = next_chunk(new_mom_in)
    new_mom_in = next_chunk(new_mom_in)
    own_1, other_1 = returns(after(inner, updates[1]), proj_out, mine, True)
    own_2, other_2 = returns(after(grad_joint, own_1), proj_in, mine, False)
    peer_all = with_other_core(peer_same)
    layer_out, back = collect(inputs, own_1, other_1, peer_same)

    new_w_in = average(updates[0], peers[0], proj_in, 0, new_w_in)
    new_mom_in = next_chunk(new_mom_in, new_w_in, *peer_all)
    new_w_out = peer_out(peer_all, peer_mine, peer_inner, peer_base, after(update_out, updates[2]))
    grad_tokens, _ = collect(upstream, own_2, other_2, back)

    new_w_in = average(updates[1], after(peers[1], new_w_out), proj_in, 1, new_w_in)
    new_mom_in = next_chunk(new_mom_in, new_w_in, layer_out)

    new_w_in = average(updates[2], peers[2], proj_in, 2, new_w_in)
    new_w_in = average(updates[3], after(peers[3], grad_tokens), proj_in, 3, new_w_in)
    return tuple(v[None] for v in (layer_out, grad_tokens, new_w_in, new_w_out, new_mom_in, new_mom_out))


def shards(tokens, cotangent, route_weight, expert_ids, slots, gossip_round, w_in, w_out, mom_in, mom_out):
    levels = lax.axis_size("rep").bit_length() - 1
    round_now = jnp.remainder(gossip_round[0], jnp.int32(levels))
    operands = [v[0] for v in (tokens, cotangent, route_weight, expert_ids, slots, w_in, w_out, mom_in, mom_out)]
    return lax.switch(round_now, [partial(step, bit=bit) for bit in range(levels)], *operands)


def solution(mesh):
    three, four = P("rep", "exp", None), P("rep", "exp", None, None)
    return jax.shard_map(
        shards,
        mesh=mesh,
        in_specs=(three, three, three, three, three, P(), four, four, four, four),
        out_specs=(three, three, four, four, four, four),
        check_vma=False,
    )
```

```python
from functools import partial
import math

import jax
import jax.numpy as jnp
from jax import lax
from jax.experimental import pallas as pl
from jax.experimental.pallas import tpu as pltpu
from jax.sharding import PartitionSpec as P

CAP = 64
MOMENTUM_DECAY = 0.9
STEP_SIZE = 0.2
COLS = 512
DEEP = 256
SCALARS = ()
PIECES = (4, 4, 9, 7)
F32 = jnp.float32
BF16 = jnp.bfloat16
VMEM = 32 * 1024 * 1024


def to_xor(value, k):
    size = lax.axis_size("exp")
    return lax.ppermute(value, "exp", [(i, i ^ k) for i in range(size)])


def swap(value):
    return to_xor(value, 1)


def along_chips(value, targets):
    return lax.ppermute(value, "exp", [(2 * c + k, 2 * t + k) for c, t in enumerate(targets) for k in range(2)])


def gossip(value, bit):
    size = lax.axis_size("rep")
    return lax.ppermute(value, "rep", [(i, i ^ (1 << bit)) for i in range(size)])


def after(value, *first):
    return lax.optimization_barrier((value, *first))[0]


def near_and_far(value):
    chips = lax.axis_size("exp") // 2
    if chips != 4:
        return [to_xor(value, 2 * s) for s in range(1, chips)]
    far = to_xor(value, 6)
    return [to_xor(value, 2), far]


def all_blocks(value, found, relayed):
    if len(found) != 2:
        return [value] + list(found)
    return [value, found[0], along_chips(relayed, (2, 0, 3, 1)), found[1]]


def with_other_core(same):
    return [part for block in same for part in (block, swap(block))]


def send_first(parts, *first):
    parts = lax.optimization_barrier((*parts, *first))[: len(parts)]
    if len(parts) != 3:
        return [to_xor(part, 2 * s + 2) for s, part in enumerate(parts)]
    return [along_chips(parts[1], (1, 3, 0, 2)), to_xor(parts[0], 2)]


def nn(a, b):
    return jnp.dot(a, b, preferred_element_type=F32)


def nt(a, b):
    return lax.dot_general(a, b, (((1,), (1,)), ((), ())), preferred_element_type=F32)


def tn(a, b):
    return lax.dot_general(a, b, (((0,), (0,)), ((), ())), preferred_element_type=F32)


def kernel_call(body, grid, ins, outs, scratch=(), flops=0, aliases=None, kept=()):
    in_hbm = pltpu.HBM

    def spec(block, where):
        if block is None:
            return pl.BlockSpec(memory_space=pl.ANY)
        if block is SCALARS:
            return pl.BlockSpec(memory_space=pltpu.SMEM)
        return pl.BlockSpec(block, where)

    moved = sum(math.prod(a.shape) * a.dtype.itemsize for a, block, _ in list(ins) + list(outs) if block is not None)
    return pl.pallas_call(
        body,
        grid=grid,
        in_specs=[spec(b, w) for _, b, w in ins],
        out_specs=[spec(b, w) for _, b, w in outs],
        out_shape=[in_hbm(a.shape, a.dtype) if k in kept else jax.ShapeDtypeStruct(a.shape, a.dtype) for k, (a, _, _) in enumerate(outs)],
        scratch_shapes=list(scratch),
        input_output_aliases=aliases or {},
        compiler_params=pltpu.CompilerParams(vmem_limit_bytes=VMEM),
        cost_estimate=pl.CostEstimate(flops=flops // 3, bytes_accessed=moved // 3, transcendentals=0),
    )(*[a for a, _, _ in ins])


def shape(dims, dtype):
    return jax.ShapeDtypeStruct(dims, dtype)


def matches(mine_ref, k, local):
    tokens = mine_ref.shape[2]
    slot = lax.broadcasted_iota(jnp.int32, (CAP, tokens), 0).astype(F32)
    return [mine_ref[k, 2 * a : 2 * a + 1, :] == slot for a in range(local)]


def onehot(found):
    return jnp.concatenate([f.astype(F32) for f in found], axis=0).astype(BF16)


def row_weights(mine_ref, k, found):
    return [
        jnp.sum(jnp.where(f, mine_ref[k, 2 * a + 1 : 2 * a + 2, :], 0.0), axis=1, keepdims=True)
        for a, f in enumerate(found)
    ]


def fill_rows(blocks, mine_ref, rows_ref, local, weighted):
    for k, block in enumerate(blocks):
        found = matches(mine_ref, k, local)
        rows = nn(onehot(found), block[...])
        weight = row_weights(mine_ref, k, found) if weighted else None
        for a in range(local):
            part = rows[a * CAP : (a + 1) * CAP]
            if weighted:
                part = part * weight[a]
            rows_ref[a, k * CAP : (k + 1) * CAP, :] = part.astype(BF16)


def forward_body(groups, local, hidden, scale, *refs):
    blocks, (mine, w, rows, inner, slope, value, joint) = refs[:groups], refs[groups:]
    fill_rows(blocks, mine, rows, local, False)
    first = pl.program_id(0) == 0

    for a in range(local):
        part = nn(rows[a], w[a])

        @pl.when(first)
        def _():
            joint[a] = part

        @pl.when(jnp.logical_not(first))
        def _():
            joint[a] += part

    @pl.when(pl.program_id(0) == pl.num_programs(0) - 1)
    def _():
        for a in range(local):
            gate = joint[a, :, :hidden] * scale
            upper = joint[a, :, hidden:] * scale
            sigmoid = jax.nn.sigmoid(gate)
            act = gate * sigmoid
            inner[a] = (act * upper).astype(BF16)
            slope[a] = upper * (sigmoid * (1.0 + gate * (1.0 - sigmoid)))
            value[a] = act


def forward(blocks, mine, proj_in):
    groups = len(blocks)
    local, width, double = proj_in.shape
    hidden, rows, tokens = double // 2, groups * CAP, blocks[0].shape[0]
    whole = lambda j: (0, 0, 0)
    return kernel_call(
        partial(forward_body, groups, local, hidden, 1.0 / math.sqrt(width)),
        (width // COLS,),
        [(b, (tokens, COLS), lambda j: (0, j)) for b in blocks]
        + [(mine, mine.shape, whole), (proj_in, (local, COLS, double), lambda j: (0, j, 0))],
        [
            (shape((local, rows, width), BF16), (local, rows, COLS), lambda j: (0, 0, j)),
            (shape((local, rows, hidden), BF16), (local, rows, hidden), whole),
            (shape((local, rows, hidden), F32), (local, rows, hidden), whole),
            (shape((local, rows, hidden), F32), (local, rows, hidden), whole),
        ],
        [pltpu.VMEM((local, rows, double), F32)],
        2 * local * rows * width * double,
    )


def backward_body(groups, local, hidden, scale, *refs):
    blocks = refs[:groups]
    mine, inner, slope, value, w, mom, new_mom, update, grad_joint, rows, grad_inner = refs[groups:]
    fill_rows(blocks, mine, rows, local, True)
    first = pl.program_id(0) == 0

    for a in range(local):
        moment = MOMENTUM_DECAY * mom[a].astype(F32) + tn(inner[a], rows[a]) * scale
        new_mom[a] = moment.astype(BF16)
        update[a] = (w[a].astype(F32) - STEP_SIZE * moment).astype(BF16)
        part = nt(rows[a], w[a])

        @pl.when(first)
        def _():
            grad_inner[a] = part

        @pl.when(jnp.logical_not(first))
        def _():
            grad_inner[a] += part

    @pl.when(pl.program_id(0) == pl.num_programs(0) - 1)
    def _():
        for a in range(local):
            grad = grad_inner[a] * scale
            grad_joint[a, :, :hidden] = (grad * slope[a]).astype(BF16)
            grad_joint[a, :, hidden:] = (grad * value[a]).astype(BF16)


def backward(blocks, mine, inner, slope, value, proj_out, mom_out):
    groups = len(blocks)
    local, hidden, width = proj_out.shape
    rows, tokens = groups * CAP, blocks[0].shape[0]
    whole = lambda j: (0, 0, 0)
    cut = ((local, hidden, COLS), lambda j: (0, 0, j))
    held = ((local, rows, hidden), whole)
    return kernel_call(
        partial(backward_body, groups, local, hidden, 1.0 / math.sqrt(hidden)),
        (width // COLS,),
        [(b, (tokens, COLS), lambda j: (0, j)) for b in blocks]
        + [(mine, mine.shape, whole), (inner, *held), (slope, *held), (value, *held), (proj_out, *cut), (mom_out, *cut)],
        [
            (proj_out, *cut),
            (proj_out, *cut),
            (shape((local, rows, 2 * hidden), BF16), (local, rows, 2 * hidden), whole),
        ],
        [pltpu.VMEM((local, rows, COLS), BF16), pltpu.VMEM((local, rows, hidden), F32)],
        4 * local * rows * width * hidden,
        kept=(0,),
    )


def peer_body(groups, local, scale, *refs):
    blocks, (mine, inner, *bases, update, new_w, rows) = refs[:groups], refs[groups:]
    fill_rows(blocks, mine, rows, local, True)
    for a in range(local):
        whole = jnp.concatenate([base[a].astype(F32) for base in bases], axis=0)
        theirs = whole - STEP_SIZE * (tn(inner[a], rows[a]) * scale)
        new_w[a] = (0.5 * (update[a].astype(F32) + theirs)).astype(BF16)


def peer_out(blocks, mine, inner, bases, update):
    groups = len(blocks)
    local, hidden, width = update.shape
    rows, tokens = groups * CAP, blocks[0].shape[0]
    whole = lambda j: (0, 0, 0)
    cut = ((local, hidden, COLS), lambda j: (0, 0, j))
    return kernel_call(
        partial(peer_body, groups, local, 1.0 / math.sqrt(hidden)),
        (width // COLS,),
        [(b, (tokens, COLS), lambda j: (0, j)) for b in blocks]
        + [(mine, mine.shape, whole), (inner, (local, rows, hidden), whole)]
        + [(b, (local, b.shape[1], COLS), lambda j: (0, 0, j)) for b in bases]
        + [(update, *cut)],
        [(update, *cut)],
        [pltpu.VMEM((local, rows, COLS), BF16)],
        2 * local * rows * width * hidden,
        kept=(0,),
    )[0]


def base_body(w, mom, *bases):
    whole = (w[...].astype(F32) - (STEP_SIZE * MOMENTUM_DECAY) * mom[...].astype(F32)).astype(BF16)
    start = 0
    for base in bases:
        base[...] = whole[:, start : start + base.shape[1]]
        start += base.shape[1]


def base_out(proj_out, mom_out):
    local, hidden, width = proj_out.shape
    cut = ((local, hidden, COLS), lambda j: (0, 0, j))
    unit = hidden // 24
    outs = [(shape((local, n * unit, width), BF16), (local, n * unit, COLS), lambda j: (0, 0, j)) for n in PIECES]
    kept = range(len(outs))
    return kernel_call(base_body, (width // COLS,), [(proj_out, *cut), (mom_out, *cut)], outs, kept=kept)


def grad_in_body(scale, rows, grad_joint, w, mom, *rest):
    update, new_mom = rest[-2:]
    moment = MOMENTUM_DECAY * mom[0].astype(F32) + tn(rows[0], grad_joint[0]) * scale
    new_mom[0] = moment.astype(BF16)
    update[0] = (w[0].astype(F32) - STEP_SIZE * moment).astype(BF16)


def grad_in(rows_in, grad_joint, proj_in, mom_in, start, depth, held):
    local, width, double = proj_in.shape
    rows = rows_in.shape[1]
    first = start // DEEP
    cut = ((1, DEEP, double), lambda a, i: (a, first + i, 0))
    ins = [
        (rows_in, (1, rows, DEEP), lambda a, i: (a, 0, first + i)),
        (grad_joint, (1, rows, double), lambda a, i: (a, 0, 0)),
        (proj_in, *cut),
        (mom_in, *cut),
    ]
    if held is not None:
        ins.append((held, None, None))
    return kernel_call(
        partial(grad_in_body, 1.0 / math.sqrt(width)),
        (local, depth // DEEP),
        ins,
        [(shape((local, depth, double), BF16), (1, DEEP, double), lambda a, i: (a, i, 0)), (proj_in, *cut)],
        flops=2 * local * rows * depth * double,
        aliases={4: 1} if held is not None else None,
        kept=(1,),
    )


def average_body(own, peer, *rest):
    rest[-1][...] = (0.5 * (own[...].astype(F32) + peer[...].astype(F32))).astype(BF16)


def average(own, peer, like, start, held):
    local, depth, double = own.shape
    block = (1, DEEP, double)
    ins = [(own, block, lambda a, i: (a, i, 0)), (peer, block, lambda a, i: (a, i, 0))]
    if held is not None:
        ins.append((held, None, None))
    return kernel_call(
        average_body,
        (local, depth // DEEP),
        ins,
        [(like, block, lambda a, i: (a, start // DEEP + i, 0))],
        aliases={2: 0} if held is not None else None,
        kept=(0,),
    )[0]


def returns_body(groups, local, scale, weighted, product, left, w, mine, own, other, rows):
    for a in range(local):
        rows[a] = (product(left[a], w[a]) * scale).astype(rows.dtype)
    for k in range(groups):
        found = matches(mine, k, local)
        weight = row_weights(mine, k, found) if weighted else None
        parts = [rows[a, k * CAP : (k + 1) * CAP, :] for a in range(local)]
        if weighted:
            parts = [p * weight[a] for a, p in enumerate(parts)]
        part = tn(onehot(found), jnp.concatenate([p.astype(BF16) for p in parts], axis=0))
        if k % 2 == 0:
            own[k // 2] = part
        else:
            other[k // 2] = part.astype(BF16)


def returns(left, w, mine, weighted):
    groups, _, tokens = mine.shape
    local, rows, inside = left.shape
    whole = lambda j: (0, 0, 0)
    if weighted:
        product, width, cut, scale = nn, w.shape[2], ((local, inside, COLS), lambda j: (0, 0, j)), 1.0 / math.sqrt(inside)
    else:
        product, width, cut, scale = nt, w.shape[1], ((local, COLS, inside), lambda j: (0, j, 0)), 1.0 / math.sqrt(w.shape[1])
    out = ((groups // 2, tokens, COLS), lambda j: (0, 0, j))
    return kernel_call(
        partial(returns_body, groups, local, scale, weighted, product),
        (width // COLS,),
        [(left, left.shape, whole), (w, *cut), (mine, mine.shape, whole)],
        [(shape((groups // 2, tokens, width), F32), *out), (shape((groups // 2, tokens, width), BF16), *out)],
        [pltpu.VMEM((local, rows, COLS), F32 if weighted else BF16)],
        2 * local * rows * width * inside,
    )


def columns(array):
    lead = array.shape[:-1]
    return array, (*lead, COLS) if lead else SCALARS, lambda j: (*(0 for _ in lead), j)


def line_end():
    chip = lax.axis_index("exp") // 2
    return ((chip == 0) | (chip == 3)).astype(jnp.int32)[None]


def by_columns(body, ins, outs, kept=()):
    return kernel_call(body, (outs[0].shape[-1] // COLS,), [columns(a) for a in ins], [columns(a) for a in outs], kept=kept)


def middle_body(ends, value, far, out):
    out[...] = jnp.where(ends[0] > 0, value[...], far[...])


def middle_of(value, found, ends):
    if len(found) != 2:
        return value
    return by_columns(middle_body, [ends, value, found[1]], [value])[0]


def paired_body(base, own, other, total, *parts):
    total[...] = base[...].astype(F32) + (own[0] + other[0].astype(F32))
    for s, part in enumerate(parts):
        part[...] = (own[s + 1] + other[s + 1].astype(F32)).astype(BF16)


def paired(base, own, other):
    out = by_columns(paired_body, [base, own, swap(other)], [shape(base.shape, F32)] + [base] * (own.shape[0] - 1))
    return out[0], out[1:]


def far_body(ends, part, middle, out):
    heard = jnp.where(ends[0] > 0, 0.0, middle[...].astype(F32))
    out[...] = (part[...].astype(F32) + heard).astype(BF16)


def send_last(parts, heard, ends):
    if len(parts) != 3:
        return heard
    far = by_columns(far_body, [ends, parts[2], heard[0]], [parts[2]])[0]
    return [*heard, to_xor(far, 6)]


def added_body(line, ends, total, *refs):
    out, heard = refs[-1], [ref[...].astype(F32) for ref in refs[:-1]]
    if line:
        heard[0] = jnp.where(ends[0] > 0, heard[0], 0.0)
    out[...] = sum(heard, total[...]).astype(BF16)


def added(total, heard, ends):
    line = lax.axis_size("exp") == 8
    return by_columns(partial(added_body, line), [ends, total, *heard], [shape(total.shape, BF16)], (0,))[0]


def routing(weights, chosen, places, local):
    groups = lax.axis_size("exp")
    tokens = chosen.shape[0]
    ids = jnp.arange(groups * local, dtype=jnp.int32)[:, None, None]
    hit = (chosen[None] == ids) & (places[None] < CAP)
    place_of = (jnp.sum(jnp.where(hit, places[None] + 1, 0), axis=2) - 1).astype(F32)
    weight_of = jnp.sum(jnp.where(hit, weights[None], 0.0), axis=2)
    packed = jnp.stack([place_of, weight_of], axis=1).reshape(groups, 2 * local, tokens)
    arrived = lax.all_to_all(packed, "exp", split_axis=0, concat_axis=0, tiled=True)
    return arrived[lax.axis_index("exp") ^ jnp.arange(groups, dtype=jnp.int32)]


def step(inputs, upstream, weights, chosen, places, proj_in, proj_out, mom_in, mom_out, bit):
    local, width, _ = proj_in.shape
    depth = 512

    ties = lax.optimization_barrier
    ends = line_end()
    first_rows = 3 * DEEP

    tok = near_and_far(inputs)
    peer_upstream = gossip(upstream, bit)
    mine = routing(weights, chosen, places, local)
    bases = base_out(proj_out, mom_out)
    peer_bases = [gossip(after(bases[0], peer_upstream), bit)]
    *tok, mine, peer_upstream, peer_bases[0] = ties((*tok, mine, peer_upstream, peer_bases[0]))
    sent = middle_of(inputs, tok, ends)
    tok_same = all_blocks(inputs, tok, sent)
    peer_bases.append(gossip(after(bases[1], sent), bit))
    peer_mine = gossip(after(mine, sent), bit)

    *tok_same, peer_bases[1], peer_mine = ties((*tok_same, peer_bases[1], peer_mine))
    upstream_now, base = ties((upstream, bases[2], *tok_same[1:], peer_bases[1]))[:2]
    cot = near_and_far(upstream_now)
    peer_bases.append(gossip(base, bit))
    rows_in, inner, slope, value = forward(with_other_core(tok_same), mine, proj_in)
    own, other = returns(inner, proj_out, mine, True)
    *cot, own, peer_bases[2] = ties((*cot, own, peer_bases[2]))
    sent = middle_of(upstream, cot, ends)
    cot_same = all_blocks(upstream, cot, sent)
    peer_inner = gossip(after(inner, sent), bit)
    total_1, parts_1 = paired(inputs, own, after(other, sent))

    *cot_same, total_1, peer_inner = ties((*cot_same, total_1, peer_inner))
    peer_bases.append(gossip(after(bases[3], peer_inner), bit))
    cot_all = with_other_core(cot_same)
    new_mom_out, update_out, grad_joint = backward(cot_all, mine, inner, slope, value, proj_out, mom_out)
    update_0, new_mom_in = grad_in(rows_in, grad_joint, proj_in, mom_in, 0, first_rows, None)
    peer_0 = gossip(update_0, bit)
    peer_upstream, new_mom_in, peer_bases[3] = ties((peer_upstream, new_mom_in, peer_bases[3]))
    heard_1 = send_first(parts_1, new_mom_in)
    there = near_and_far(peer_upstream)
    last = width - DEEP
    update_1, new_mom_in = grad_in(rows_in, grad_joint, proj_in, mom_in, first_rows, last - first_rows, new_mom_in)
    peer_1 = gossip(update_1, bit)
    update_2, new_mom_in = grad_in(rows_in, grad_joint, proj_in, mom_in, last, DEEP, new_mom_in)
    peer_2 = gossip(update_2, bit)
    own, other = returns(after(grad_joint, update_2), proj_in, mine, False)

    *there, own, heard_1[0] = ties((*there, own, *heard_1))[: len(there) + 2]
    heard_1 = send_last(parts_1, heard_1, ends)
    sent = middle_of(peer_upstream, there, ends)
    there_same = all_blocks(peer_upstream, there, sent)
    total_2, parts_2 = paired(upstream, own, after(other, sent))
    new_w_in = average(update_0, after(peer_0, total_2), proj_in, 0, None)

    *there_same, new_w_in, heard_1[-1] = ties((*there_same, new_w_in, heard_1[-1]))
    layer_out = added(total_1, heard_1, ends)
    heard_2 = send_first(parts_2, there_same[2])
    there_all = with_other_core(there_same)
    new_w_out = peer_out(there_all, peer_mine, peer_inner, peer_bases, update_out)
    *heard_2, new_w_out, layer_out = ties((*heard_2, new_w_out, layer_out))
    grad_tokens = added(total_2, send_last(parts_2, heard_2, ends), ends)

    new_w_in = average(update_1, after(peer_1, grad_tokens), proj_in, first_rows, new_w_in)
    new_w_in = average(update_2, peer_2, proj_in, last, new_w_in)
    return tuple(v[None] for v in (layer_out, grad_tokens, new_w_in, new_w_out, new_mom_in, new_mom_out))


def shards(tokens, cotangent, route_weight, expert_ids, slots, gossip_round, w_in, w_out, mom_in, mom_out):
    levels = lax.axis_size("rep").bit_length() - 1
    round_now = jnp.remainder(gossip_round[0], jnp.int32(levels))
    operands = [v[0] for v in (tokens, cotangent, route_weight, expert_ids, slots, w_in, w_out, mom_in, mom_out)]
    return lax.switch(round_now, [partial(step, bit=bit) for bit in range(levels)], *operands)


def solution(mesh):
    three, four = P("rep", "exp", None), P("rep", "exp", None, None)
    return jax.shard_map(
        shards,
        mesh=mesh,
        in_specs=(three, three, three, three, three, P(), four, four, four, four),
        out_specs=(three, three, four, four, four, four),
        check_vma=False,
    )
```

```python
from functools import partial
import math

import jax
import jax.numpy as jnp
from jax import lax
from jax.experimental import pallas as pl
from jax.experimental.pallas import tpu as pltpu
from jax.sharding import PartitionSpec as P

CAP = 64
MOMENTUM_DECAY = 0.9
STEP_SIZE = 0.2
COLS = 512
DEEP = 256
SCALARS = ()
PIECES = (4, 4, 11, 5)
F32 = jnp.float32
BF16 = jnp.bfloat16
VMEM = 32 * 1024 * 1024


def to_xor(value, k):
    size = lax.axis_size("exp")
    return lax.ppermute(value, "exp", [(i, i ^ k) for i in range(size)])


def swap(value):
    return to_xor(value, 1)


def along_chips(value, targets):
    return lax.ppermute(value, "exp", [(2 * c + k, 2 * t + k) for c, t in enumerate(targets) for k in range(2)])


def gossip(value, bit):
    size = lax.axis_size("rep")
    return lax.ppermute(value, "rep", [(i, i ^ (1 << bit)) for i in range(size)])


def after(value, *first):
    return lax.optimization_barrier((value, *first))[0]


def near_and_far(value):
    chips = lax.axis_size("exp") // 2
    if chips != 4:
        return [to_xor(value, 2 * s) for s in range(1, chips)]
    far = to_xor(value, 6)
    return [to_xor(value, 2), far]


def all_blocks(value, found, relayed):
    if len(found) != 2:
        return [value] + list(found)
    return [value, found[0], along_chips(relayed, (2, 0, 3, 1)), found[1]]


def with_other_core(same):
    return [part for block in same for part in (block, swap(block))]


def send_first(parts, *first):
    parts = lax.optimization_barrier((*parts, *first))[: len(parts)]
    if len(parts) != 3:
        return [to_xor(part, 2 * s + 2) for s, part in enumerate(parts)]
    return [along_chips(parts[1], (1, 3, 0, 2)), to_xor(parts[0], 2)]


def nn(a, b):
    return jnp.dot(a, b, preferred_element_type=F32)


def nt(a, b):
    return lax.dot_general(a, b, (((1,), (1,)), ((), ())), preferred_element_type=F32)


def tn(a, b):
    return lax.dot_general(a, b, (((0,), (0,)), ((), ())), preferred_element_type=F32)


def kernel_call(body, grid, ins, outs, scratch=(), flops=0, aliases=None, kept=()):
    in_hbm = pltpu.HBM

    def spec(block, where):
        if block is None:
            return pl.BlockSpec(memory_space=pl.ANY)
        if block is SCALARS:
            return pl.BlockSpec(memory_space=pltpu.SMEM)
        return pl.BlockSpec(block, where)

    moved = sum(math.prod(a.shape) * a.dtype.itemsize for a, block, _ in list(ins) + list(outs) if block is not None)
    return pl.pallas_call(
        body,
        grid=grid,
        in_specs=[spec(b, w) for _, b, w in ins],
        out_specs=[spec(b, w) for _, b, w in outs],
        out_shape=[in_hbm(a.shape, a.dtype) if k in kept else jax.ShapeDtypeStruct(a.shape, a.dtype) for k, (a, _, _) in enumerate(outs)],
        scratch_shapes=list(scratch),
        input_output_aliases=aliases or {},
        compiler_params=pltpu.CompilerParams(vmem_limit_bytes=VMEM),
        cost_estimate=pl.CostEstimate(flops=flops // 3, bytes_accessed=moved // 3, transcendentals=0),
    )(*[a for a, _, _ in ins])


def shape(dims, dtype):
    return jax.ShapeDtypeStruct(dims, dtype)


def matches(mine_ref, k, local):
    tokens = mine_ref.shape[2]
    slot = lax.broadcasted_iota(jnp.int32, (CAP, tokens), 0).astype(F32)
    return [mine_ref[k, 2 * a : 2 * a + 1, :] == slot for a in range(local)]


def onehot(found):
    return jnp.concatenate([f.astype(F32) for f in found], axis=0).astype(BF16)


def row_weights(mine_ref, k, found):
    return [
        jnp.sum(jnp.where(f, mine_ref[k, 2 * a + 1 : 2 * a + 2, :], 0.0), axis=1, keepdims=True)
        for a, f in enumerate(found)
    ]


def fill_rows(blocks, mine_ref, rows_ref, local, weighted):
    for k, block in enumerate(blocks):
        found = matches(mine_ref, k, local)
        rows = nn(onehot(found), block[...])
        weight = row_weights(mine_ref, k, found) if weighted else None
        for a in range(local):
            part = rows[a * CAP : (a + 1) * CAP]
            if weighted:
                part = part * weight[a]
            rows_ref[a, k * CAP : (k + 1) * CAP, :] = part.astype(BF16)


def forward_body(groups, local, hidden, scale, *refs):
    blocks, (mine, w, turned, inner, turned_inner, slope, value, joint, rows) = refs[:groups], refs[groups:]
    fill_rows(blocks, mine, rows, local, False)
    first = pl.program_id(0) == 0

    for a in range(local):
        turned[a] = rows[a].T
        part = nn(rows[a], w[a])

        @pl.when(first)
        def _():
            joint[a] = part

        @pl.when(jnp.logical_not(first))
        def _():
            joint[a] += part

    @pl.when(pl.program_id(0) == pl.num_programs(0) - 1)
    def _():
        for a in range(local):
            gate = joint[a, :, :hidden] * scale
            upper = joint[a, :, hidden:] * scale
            sigmoid = jax.nn.sigmoid(gate)
            act = gate * sigmoid
            inner[a] = (act * upper).astype(BF16)
            turned_inner[a] = inner[a].T
            slope[a] = upper * (sigmoid * (1.0 + gate * (1.0 - sigmoid)))
            value[a] = act


def forward(blocks, mine, proj_in):
    groups = len(blocks)
    local, width, double = proj_in.shape
    hidden, rows, tokens = double // 2, groups * CAP, blocks[0].shape[0]
    whole = lambda j: (0, 0, 0)
    return kernel_call(
        partial(forward_body, groups, local, hidden, 1.0 / math.sqrt(width)),
        (width // COLS,),
        [(b, (tokens, COLS), lambda j: (0, j)) for b in blocks]
        + [(mine, mine.shape, whole), (proj_in, (local, COLS, double), lambda j: (0, j, 0))],
        [
            (shape((local, width, rows), BF16), (local, COLS, rows), lambda j: (0, j, 0)),
            (shape((local, rows, hidden), BF16), (local, rows, hidden), whole),
            (shape((local, hidden, rows), BF16), (local, hidden, rows), whole),
            (shape((local, rows, hidden), F32), (local, rows, hidden), whole),
            (shape((local, rows, hidden), F32), (local, rows, hidden), whole),
        ],
        [pltpu.VMEM((local, rows, double), F32), pltpu.VMEM((local, rows, COLS), BF16)],
        2 * local * rows * width * double,
    )


def backward_body(groups, local, hidden, scale, *refs):
    blocks = refs[:groups]
    mine, turned_inner, slope, value, w, mom, new_mom, update, grad_joint, rows, grad_inner = refs[groups:]
    fill_rows(blocks, mine, rows, local, True)
    first = pl.program_id(0) == 0

    for a in range(local):
        moment = MOMENTUM_DECAY * mom[a].astype(F32) + nn(turned_inner[a], rows[a]) * scale
        new_mom[a] = moment.astype(BF16)
        update[a] = (w[a].astype(F32) - STEP_SIZE * moment).astype(BF16)
        part = nt(rows[a], w[a])

        @pl.when(first)
        def _():
            grad_inner[a] = part

        @pl.when(jnp.logical_not(first))
        def _():
            grad_inner[a] += part

    @pl.when(pl.program_id(0) == pl.num_programs(0) - 1)
    def _():
        for a in range(local):
            grad = grad_inner[a] * scale
            grad_joint[a, :, :hidden] = (grad * slope[a]).astype(BF16)
            grad_joint[a, :, hidden:] = (grad * value[a]).astype(BF16)


def backward(blocks, mine, turned_inner, slope, value, proj_out, mom_out):
    groups = len(blocks)
    local, hidden, width = proj_out.shape
    rows, tokens = groups * CAP, blocks[0].shape[0]
    whole = lambda j: (0, 0, 0)
    cut = ((local, hidden, COLS), lambda j: (0, 0, j))
    held = ((local, rows, hidden), whole)
    return kernel_call(
        partial(backward_body, groups, local, hidden, 1.0 / math.sqrt(hidden)),
        (width // COLS,),
        [(b, (tokens, COLS), lambda j: (0, j)) for b in blocks]
        + [(mine, mine.shape, whole), (turned_inner, (local, hidden, rows), whole), (slope, *held), (value, *held), (proj_out, *cut), (mom_out, *cut)],
        [
            (proj_out, *cut),
            (proj_out, *cut),
            (shape((local, rows, 2 * hidden), BF16), (local, rows, 2 * hidden), whole),
        ],
        [pltpu.VMEM((local, rows, COLS), BF16), pltpu.VMEM((local, rows, hidden), F32)],
        4 * local * rows * width * hidden,
        kept=(0,),
    )


def peer_body(groups, local, scale, *refs):
    blocks, (mine, turned_inner, *bases, update, new_w, rows) = refs[:groups], refs[groups:]
    fill_rows(blocks, mine, rows, local, True)
    for a in range(local):
        whole = jnp.concatenate([base[a].astype(F32) for base in bases], axis=0)
        theirs = whole - STEP_SIZE * (nn(turned_inner[a], rows[a]) * scale)
        new_w[a] = (0.5 * (update[a].astype(F32) + theirs)).astype(BF16)


def peer_out(blocks, mine, turned_inner, bases, update):
    groups = len(blocks)
    local, hidden, width = update.shape
    rows, tokens = groups * CAP, blocks[0].shape[0]
    whole = lambda j: (0, 0, 0)
    cut = ((local, hidden, COLS), lambda j: (0, 0, j))
    return kernel_call(
        partial(peer_body, groups, local, 1.0 / math.sqrt(hidden)),
        (width // COLS,),
        [(b, (tokens, COLS), lambda j: (0, j)) for b in blocks]
        + [(mine, mine.shape, whole), (turned_inner, (local, hidden, rows), whole)]
        + [(b, (local, b.shape[1], COLS), lambda j: (0, 0, j)) for b in bases]
        + [(update, *cut)],
        [(update, *cut)],
        [pltpu.VMEM((local, rows, COLS), BF16)],
        2 * local * rows * width * hidden,
        kept=(0,),
    )[0]


def base_body(w, mom, *bases):
    whole = (w[...].astype(F32) - (STEP_SIZE * MOMENTUM_DECAY) * mom[...].astype(F32)).astype(BF16)
    start = 0
    for base in bases:
        base[...] = whole[:, start : start + base.shape[1]]
        start += base.shape[1]


def base_out(proj_out, mom_out):
    local, hidden, width = proj_out.shape
    cut = ((local, hidden, COLS), lambda j: (0, 0, j))
    unit = hidden // 24
    outs = [(shape((local, n * unit, width), BF16), (local, n * unit, COLS), lambda j: (0, 0, j)) for n in PIECES]
    kept = range(len(outs))
    return kernel_call(base_body, (width // COLS,), [(proj_out, *cut), (mom_out, *cut)], outs, kept=kept)


def grad_in_body(scale, turned, grad_joint, w, mom, *rest):
    update, new_mom = rest[-2:]
    moment = MOMENTUM_DECAY * mom[0].astype(F32) + nn(turned[0], grad_joint[0]) * scale
    new_mom[0] = moment.astype(BF16)
    update[0] = (w[0].astype(F32) - STEP_SIZE * moment).astype(BF16)


def grad_in(turned_rows, grad_joint, proj_in, mom_in, start, depth, held):
    local, width, double = proj_in.shape
    rows = turned_rows.shape[2]
    first = start // DEEP
    cut = ((1, DEEP, double), lambda a, i: (a, first + i, 0))
    ins = [
        (turned_rows, (1, DEEP, rows), lambda a, i: (a, first + i, 0)),
        (grad_joint, (1, rows, double), lambda a, i: (a, 0, 0)),
        (proj_in, *cut),
        (mom_in, *cut),
    ]
    if held is not None:
        ins.append((held, None, None))
    return kernel_call(
        partial(grad_in_body, 1.0 / math.sqrt(width)),
        (local, depth // DEEP),
        ins,
        [(shape((local, depth, double), BF16), (1, DEEP, double), lambda a, i: (a, i, 0)), (proj_in, *cut)],
        flops=2 * local * rows * depth * double,
        aliases={4: 1} if held is not None else None,
        kept=(1,),
    )


def average_body(own, peer, *rest):
    rest[-1][...] = (0.5 * (own[...].astype(F32) + peer[...].astype(F32))).astype(BF16)


def average(own, peer, like, start, held):
    local, depth, double = own.shape
    block = (1, DEEP, double)
    ins = [(own, block, lambda a, i: (a, i, 0)), (peer, block, lambda a, i: (a, i, 0))]
    if held is not None:
        ins.append((held, None, None))
    return kernel_call(
        average_body,
        (local, depth // DEEP),
        ins,
        [(like, block, lambda a, i: (a, start // DEEP + i, 0))],
        aliases={2: 0} if held is not None else None,
        kept=(0,),
    )[0]


def returns_body(groups, local, scale, weighted, product, left, w, mine, own, other, rows):
    for a in range(local):
        rows[a] = (product(left[a], w[a]) * scale).astype(rows.dtype)
    for k in range(groups):
        found = matches(mine, k, local)
        weight = row_weights(mine, k, found) if weighted else None
        parts = [rows[a, k * CAP : (k + 1) * CAP, :] for a in range(local)]
        if weighted:
            parts = [p * weight[a] for a, p in enumerate(parts)]
        part = tn(onehot(found), jnp.concatenate([p.astype(BF16) for p in parts], axis=0))
        if k % 2 == 0:
            own[k // 2] = part
        else:
            other[k // 2] = part.astype(BF16)


def returns(left, w, mine, weighted):
    groups, _, tokens = mine.shape
    local, rows, inside = left.shape
    whole = lambda j: (0, 0, 0)
    if weighted:
        product, width, cut, scale = nn, w.shape[2], ((local, inside, COLS), lambda j: (0, 0, j)), 1.0 / math.sqrt(inside)
    else:
        product, width, cut, scale = nt, w.shape[1], ((local, COLS, inside), lambda j: (0, j, 0)), 1.0 / math.sqrt(w.shape[1])
    out = ((groups // 2, tokens, COLS), lambda j: (0, 0, j))
    return kernel_call(
        partial(returns_body, groups, local, scale, weighted, product),
        (width // COLS,),
        [(left, left.shape, whole), (w, *cut), (mine, mine.shape, whole)],
        [(shape((groups // 2, tokens, width), F32), *out), (shape((groups // 2, tokens, width), BF16), *out)],
        [pltpu.VMEM((local, rows, COLS), F32 if weighted else BF16)],
        2 * local * rows * width * inside,
    )


def columns(array):
    lead = array.shape[:-1]
    return array, (*lead, COLS) if lead else SCALARS, lambda j: (*(0 for _ in lead), j)


def line_end():
    chip = lax.axis_index("exp") // 2
    return ((chip == 0) | (chip == 3)).astype(jnp.int32)[None]


def by_columns(body, ins, outs, kept=()):
    return kernel_call(body, (outs[0].shape[-1] // COLS,), [columns(a) for a in ins], [columns(a) for a in outs], kept=kept)


def middle_body(ends, value, far, out):
    out[...] = jnp.where(ends[0] > 0, value[...], far[...])


def middle_of(value, found, ends):
    if len(found) != 2:
        return value
    return by_columns(middle_body, [ends, value, found[1]], [value])[0]


def paired_body(base, own, other, total, *parts):
    total[...] = base[...].astype(F32) + (own[0] + other[0].astype(F32))
    for s, part in enumerate(parts):
        part[...] = (own[s + 1] + other[s + 1].astype(F32)).astype(BF16)


def paired(base, own, other):
    out = by_columns(paired_body, [base, own, swap(other)], [shape(base.shape, F32)] + [base] * (own.shape[0] - 1))
    return out[0], out[1:]


def far_body(ends, part, middle, out):
    heard = jnp.where(ends[0] > 0, 0.0, middle[...].astype(F32))
    out[...] = (part[...].astype(F32) + heard).astype(BF16)


def send_last(parts, heard, ends):
    if len(parts) != 3:
        return heard
    far = by_columns(far_body, [ends, parts[2], heard[0]], [parts[2]])[0]
    return [*heard, to_xor(far, 6)]


def added_body(line, ends, total, *refs):
    out, heard = refs[-1], [ref[...].astype(F32) for ref in refs[:-1]]
    if line:
        heard[0] = jnp.where(ends[0] > 0, heard[0], 0.0)
    out[...] = sum(heard, total[...]).astype(BF16)


def added(total, heard, ends):
    line = lax.axis_size("exp") == 8
    return by_columns(partial(added_body, line), [ends, total, *heard], [shape(total.shape, BF16)], (0,))[0]


def routing(weights, chosen, places, local):
    groups = lax.axis_size("exp")
    tokens = chosen.shape[0]
    ids = jnp.arange(groups * local, dtype=jnp.int32)[:, None, None]
    hit = (chosen[None] == ids) & (places[None] < CAP)
    place_of = (jnp.sum(jnp.where(hit, places[None] + 1, 0), axis=2) - 1).astype(F32)
    weight_of = jnp.sum(jnp.where(hit, weights[None], 0.0), axis=2)
    packed = jnp.stack([place_of, weight_of], axis=1).reshape(groups, 2 * local, tokens)
    arrived = lax.all_to_all(packed, "exp", split_axis=0, concat_axis=0, tiled=True)
    return arrived[lax.axis_index("exp") ^ jnp.arange(groups, dtype=jnp.int32)]


def step(inputs, upstream, weights, chosen, places, proj_in, proj_out, mom_in, mom_out, bit):
    local, width, _ = proj_in.shape
    depth = 512

    ties = lax.optimization_barrier
    ends = line_end()
    first_rows = 3 * DEEP

    tok = near_and_far(inputs)
    peer_upstream = gossip(upstream, bit)
    mine = routing(weights, chosen, places, local)
    bases = base_out(proj_out, mom_out)
    peer_bases = [gossip(after(bases[0], peer_upstream), bit)]
    *tok, mine, peer_upstream, peer_bases[0] = ties((*tok, mine, peer_upstream, peer_bases[0]))
    sent = middle_of(inputs, tok, ends)
    tok_same = all_blocks(inputs, tok, sent)
    peer_bases.append(gossip(after(bases[1], sent), bit))
    peer_mine = gossip(after(mine, sent), bit)

    *tok_same, peer_bases[1], peer_mine = ties((*tok_same, peer_bases[1], peer_mine))
    upstream_now, base = ties((upstream, bases[2], *tok_same[1:], peer_bases[1]))[:2]
    cot = near_and_far(upstream_now)
    peer_bases.append(gossip(base, bit))
    turned_rows, inner, turned_inner, slope, value = forward(with_other_core(tok_same), mine, proj_in)
    own, other = returns(inner, proj_out, mine, True)
    *cot, own, peer_bases[2] = ties((*cot, own, peer_bases[2]))
    sent = middle_of(upstream, cot, ends)
    cot_same = all_blocks(upstream, cot, sent)
    peer_bases.append(gossip(after(bases[3], sent), bit))
    total_1, parts_1 = paired(inputs, own, after(other, sent))

    early = [0, 1, 3] if len(cot_same) == 4 else []
    swapped = {s: swap(cot_same[s]) for s in early}
    *cot_same, total_1, peer_bases[3], swapped = ties((*cot_same, total_1, peer_bases[3], swapped))
    peer_inner = gossip(after(turned_inner, peer_bases[3]), bit)
    cot_all = [part for s, block in enumerate(cot_same) for part in (block, swapped[s] if s in swapped else swap(block))]
    new_mom_out, update_out, grad_joint = backward(cot_all, mine, turned_inner, slope, value, proj_out, mom_out)
    update_0, new_mom_in = grad_in(turned_rows, grad_joint, proj_in, mom_in, 0, first_rows, None)
    peer_0 = gossip(update_0, bit)
    new_mom_in, peer_inner = ties((new_mom_in, peer_inner))
    heard_1 = send_first(parts_1, cot_same[2])
    there = near_and_far(after(peer_upstream, cot_same[2]))
    last = width - DEEP
    update_1, new_mom_in = grad_in(turned_rows, grad_joint, proj_in, mom_in, first_rows, last - first_rows, new_mom_in)
    peer_1 = gossip(update_1, bit)
    update_2, new_mom_in = grad_in(turned_rows, grad_joint, proj_in, mom_in, last, DEEP, new_mom_in)
    peer_2 = gossip(update_2, bit)
    own, other = returns(after(grad_joint, update_2), proj_in, mine, False)

    *there, own, heard_1[0] = ties((*there, own, *heard_1))[: len(there) + 2]
    heard_1 = send_last(parts_1, heard_1, ends)
    sent = middle_of(peer_upstream, there, ends)
    there_same = all_blocks(peer_upstream, there, sent)
    total_2, parts_2 = paired(upstream, own, after(other, sent))
    new_w_in = average(update_0, after(peer_0, total_2), proj_in, 0, None)

    *there_same, new_w_in, heard_1[-1] = ties((*there_same, new_w_in, heard_1[-1]))
    layer_out = added(total_1, heard_1, ends)
    heard_2 = send_first(parts_2, there_same[2])
    there_all = with_other_core(there_same)
    new_w_out = peer_out(there_all, peer_mine, peer_inner, peer_bases, update_out)
    *heard_2, new_w_out, layer_out = ties((*heard_2, new_w_out, layer_out))
    grad_tokens = added(total_2, send_last(parts_2, heard_2, ends), ends)

    new_w_in = average(update_1, after(peer_1, grad_tokens), proj_in, first_rows, new_w_in)
    new_w_in = average(update_2, peer_2, proj_in, last, new_w_in)
    return tuple(v[None] for v in (layer_out, grad_tokens, new_w_in, new_w_out, new_mom_in, new_mom_out))


def shards(tokens, cotangent, route_weight, expert_ids, slots, gossip_round, w_in, w_out, mom_in, mom_out):
    levels = lax.axis_size("rep").bit_length() - 1
    round_now = jnp.remainder(gossip_round[0], jnp.int32(levels))
    operands = [v[0] for v in (tokens, cotangent, route_weight, expert_ids, slots, w_in, w_out, mom_in, mom_out)]
    return lax.switch(round_now, [partial(step, bit=bit) for bit in range(levels)], *operands)


def solution(mesh):
    three, four = P("rep", "exp", None), P("rep", "exp", None, None)
    return jax.shard_map(
        shards,
        mesh=mesh,
        in_specs=(three, three, three, three, three, P(), four, four, four, four),
        out_specs=(three, three, four, four, four, four),
        check_vma=False,
    )
```

```python
from functools import partial
import math

import jax
import jax.numpy as jnp
from jax import lax
from jax.experimental import pallas as pl
from jax.experimental.pallas import tpu as pltpu
from jax.sharding import PartitionSpec as P

CAP = 64
MOMENTUM_DECAY = 0.9
STEP_SIZE = 0.2
COLS = 512
DEEP = 256
SCALARS = ()
PIECES = (4, 4, 10, 4)
LAST_PIECE = 2
F32 = jnp.float32
BF16 = jnp.bfloat16
VMEM = 32 * 1024 * 1024


def to_xor(value, k):
    size = lax.axis_size("exp")
    return lax.ppermute(value, "exp", [(i, i ^ k) for i in range(size)])


def swap(value):
    return to_xor(value, 1)


def along_chips(value, targets):
    return lax.ppermute(value, "exp", [(2 * c + k, 2 * t + k) for c, t in enumerate(targets) for k in range(2)])


def gossip(value, bit):
    size = lax.axis_size("rep")
    return lax.ppermute(value, "rep", [(i, i ^ (1 << bit)) for i in range(size)])


def after(value, *first):
    return lax.optimization_barrier((value, *first))[0]


def near_and_far(value):
    chips = lax.axis_size("exp") // 2
    if chips != 4:
        return [to_xor(value, 2 * s) for s in range(1, chips)]
    far = to_xor(value, 6)
    return [to_xor(value, 2), far]


def all_blocks(value, found, relayed):
    if len(found) != 2:
        return [value] + list(found)
    return [value, found[0], along_chips(relayed, (2, 0, 3, 1)), found[1]]


def with_other_core(same):
    return [part for block in same for part in (block, swap(block))]


def send_first(parts, *first):
    parts = lax.optimization_barrier((*parts, *first))[: len(parts)]
    if len(parts) != 3:
        return [to_xor(part, 2 * s + 2) for s, part in enumerate(parts)]
    return [along_chips(parts[1], (1, 3, 0, 2)), to_xor(parts[0], 2)]


def nn(a, b):
    return jnp.dot(a, b, preferred_element_type=F32)


def nt(a, b):
    return lax.dot_general(a, b, (((1,), (1,)), ((), ())), preferred_element_type=F32)


def tn(a, b):
    return lax.dot_general(a, b, (((0,), (0,)), ((), ())), preferred_element_type=F32)


def kernel_call(body, grid, ins, outs, scratch=(), flops=0, aliases=None, kept=()):
    in_hbm = pltpu.HBM

    def spec(block, where):
        if block is None:
            return pl.BlockSpec(memory_space=pl.ANY)
        if block is SCALARS:
            return pl.BlockSpec(memory_space=pltpu.SMEM)
        return pl.BlockSpec(block, where)

    moved = sum(math.prod(a.shape) * a.dtype.itemsize for a, block, _ in list(ins) + list(outs) if block is not None)
    return pl.pallas_call(
        body,
        grid=grid,
        in_specs=[spec(b, w) for _, b, w in ins],
        out_specs=[spec(b, w) for _, b, w in outs],
        out_shape=[in_hbm(a.shape, a.dtype) if k in kept else jax.ShapeDtypeStruct(a.shape, a.dtype) for k, (a, _, _) in enumerate(outs)],
        scratch_shapes=list(scratch),
        input_output_aliases=aliases or {},
        compiler_params=pltpu.CompilerParams(vmem_limit_bytes=VMEM),
        cost_estimate=pl.CostEstimate(flops=flops, bytes_accessed=moved, transcendentals=0),
    )(*[a for a, _, _ in ins])


def shape(dims, dtype):
    return jax.ShapeDtypeStruct(dims, dtype)


def matches(mine_ref, k, local):
    tokens = mine_ref.shape[2]
    slot = lax.broadcasted_iota(jnp.int32, (CAP, tokens), 0).astype(F32)
    return [mine_ref[k, 2 * a : 2 * a + 1, :] == slot for a in range(local)]


def kept_routing(groups, local, tokens, weighted):
    hot = pltpu.VMEM((groups, local * CAP, tokens), BF16)
    return [hot, pltpu.VMEM((groups, local * CAP, 1), F32)] if weighted else [hot]


def find_rows(mine_ref, local, hot, weight=None):
    @pl.when(pl.program_id(0) == 0)
    def _():
        for k in range(hot.shape[0]):
            found = matches(mine_ref, k, local)
            hot[k] = jnp.concatenate([f.astype(F32) for f in found], axis=0).astype(BF16)
            if weight is not None:
                one = [
                    jnp.sum(jnp.where(f, mine_ref[k, 2 * a + 1 : 2 * a + 2, :], 0.0), axis=1, keepdims=True)
                    for a, f in enumerate(found)
                ]
                weight[k] = jnp.concatenate(one, axis=0)


def fill_rows(blocks, mine_ref, rows_ref, local, hot, weight=None):
    find_rows(mine_ref, local, hot, weight)
    for k, block in enumerate(blocks):
        rows = nn(hot[k], block[...])
        if weight is not None:
            rows = rows * weight[k]
        for a in range(local):
            rows_ref[a, k * CAP : (k + 1) * CAP, :] = rows[a * CAP : (a + 1) * CAP].astype(BF16)


def forward_body(groups, local, hidden, scale, *refs):
    blocks, (mine, w, last_w, last_mom, turned, inner, packet, slope, value, joint, rows, hot) = refs[:groups], refs[groups:]
    base = (last_w[...].astype(F32) - (STEP_SIZE * MOMENTUM_DECAY) * last_mom[...].astype(F32)).astype(BF16)
    packet[:, last_rows(hidden, base.shape[1]), : base.shape[2]] = base
    fill_rows(blocks, mine, rows, local, hot)
    first = pl.program_id(0) == 0

    for a in range(local):
        turned[a] = rows[a].T
        part = nn(rows[a], w[a])

        @pl.when(first)
        def _():
            joint[a] = part

        @pl.when(jnp.logical_not(first))
        def _():
            joint[a] += part

    @pl.when(pl.program_id(0) == pl.num_programs(0) - 1)
    def _():
        for a in range(local):
            gate = joint[a, :, :hidden] * scale
            upper = joint[a, :, hidden:] * scale
            sigmoid = jax.nn.sigmoid(gate)
            act = gate * sigmoid
            inner[a] = (act * upper).astype(BF16)
            packet[a, :hidden] = inner[a].T
            slope[a] = upper * (sigmoid * (1.0 + gate * (1.0 - sigmoid)))
            value[a] = act


def last_rows(hidden, size):
    return pl.ds(pl.multiple_of(hidden + pl.program_id(0) * size, size), size)


def forward(blocks, mine, proj_in, proj_out, mom_out):
    groups = len(blocks)
    local, width, double = proj_in.shape
    hidden, rows, tokens = double // 2, groups * CAP, blocks[0].shape[0]
    last = hidden // 24 * LAST_PIECE
    tall = hidden + last * (width // COLS)
    whole = lambda j: (0, 0, 0)
    return kernel_call(
        partial(forward_body, groups, local, hidden, 1.0 / math.sqrt(width)),
        (width // COLS,),
        [(b, (tokens, COLS), lambda j: (0, j)) for b in blocks]
        + [(mine, mine.shape, whole), (proj_in, (local, COLS, double), lambda j: (0, j, 0))]
        + [(v, (local, last, COLS), lambda j: (0, hidden // last - 1, j)) for v in (proj_out, mom_out)],
        [
            (shape((local, width, rows), BF16), (local, COLS, rows), lambda j: (0, j, 0)),
            (shape((local, rows, hidden), BF16), (local, rows, hidden), whole),
            (shape((local, tall, rows), BF16), (local, tall, rows), whole),
            (shape((local, rows, hidden), F32), (local, rows, hidden), whole),
            (shape((local, rows, hidden), F32), (local, rows, hidden), whole),
        ],
        [pltpu.VMEM((local, rows, double), F32), pltpu.VMEM((local, rows, COLS), BF16)]
        + kept_routing(groups, local, tokens, False),
        2 * local * rows * width * double,
    )


def backward_body(groups, local, hidden, scale, *refs):
    blocks = refs[:groups]
    mine, turned_inner, slope, value, w, mom, new_mom, update, grad_joint, rows, grad_inner, hot, weight = refs[groups:]
    fill_rows(blocks, mine, rows, local, hot, weight)
    first = pl.program_id(0) == 0

    for a in range(local):
        moment = MOMENTUM_DECAY * mom[a].astype(F32) + nn(turned_inner[a], rows[a]) * scale
        new_mom[a] = moment.astype(BF16)
        update[a] = (w[a].astype(F32) - STEP_SIZE * moment).astype(BF16)
        part = nt(rows[a], w[a])

        @pl.when(first)
        def _():
            grad_inner[a] = part

        @pl.when(jnp.logical_not(first))
        def _():
            grad_inner[a] += part

    @pl.when(pl.program_id(0) == pl.num_programs(0) - 1)
    def _():
        for a in range(local):
            grad = grad_inner[a] * scale
            grad_joint[a, :, :hidden] = (grad * slope[a]).astype(BF16)
            grad_joint[a, :, hidden:] = (grad * value[a]).astype(BF16)


def backward(blocks, mine, turned_inner, slope, value, proj_out, mom_out):
    groups = len(blocks)
    local, hidden, width = proj_out.shape
    rows, tokens = groups * CAP, blocks[0].shape[0]
    whole = lambda j: (0, 0, 0)
    cut = ((local, hidden, COLS), lambda j: (0, 0, j))
    held = ((local, rows, hidden), whole)
    return kernel_call(
        partial(backward_body, groups, local, hidden, 1.0 / math.sqrt(hidden)),
        (width // COLS,),
        [(b, (tokens, COLS), lambda j: (0, j)) for b in blocks]
        + [(mine, mine.shape, whole), (turned_inner, (local, hidden, rows), whole), (slope, *held), (value, *held), (proj_out, *cut), (mom_out, *cut)],
        [
            (proj_out, *cut),
            (proj_out, *cut),
            (shape((local, rows, 2 * hidden), BF16), (local, rows, 2 * hidden), whole),
        ],
        [pltpu.VMEM((local, rows, COLS), BF16), pltpu.VMEM((local, rows, hidden), F32)]
        + kept_routing(groups, local, tokens, True),
        4 * local * rows * width * hidden,
        kept=(0,),
    )


def peer_body(groups, local, scale, *refs):
    blocks, (mine, packet, *bases, update, new_w, rows, hot, weight) = refs[:groups], refs[groups:]
    hidden, width = update.shape[1:]
    last = hidden - sum(base.shape[1] for base in bases)
    fill_rows(blocks, mine, rows, local, hot, weight)
    for a in range(local):
        below = packet[a, last_rows(hidden, last), :width]
        whole = jnp.concatenate([base[a].astype(F32) for base in bases] + [below.astype(F32)], axis=0)
        theirs = whole - STEP_SIZE * (nn(packet[a, :hidden], rows[a]) * scale)
        new_w[a] = (0.5 * (update[a].astype(F32) + theirs)).astype(BF16)


def peer_out(blocks, mine, packet, bases, update):
    groups = len(blocks)
    local, hidden, width = update.shape
    rows, tokens = groups * CAP, blocks[0].shape[0]
    whole = lambda j: (0, 0, 0)
    cut = ((local, hidden, COLS), lambda j: (0, 0, j))
    return kernel_call(
        partial(peer_body, groups, local, 1.0 / math.sqrt(hidden)),
        (width // COLS,),
        [(b, (tokens, COLS), lambda j: (0, j)) for b in blocks]
        + [(mine, mine.shape, whole), (packet, packet.shape, whole)]
        + [(b, (local, b.shape[1], COLS), lambda j: (0, 0, j)) for b in bases]
        + [(update, *cut)],
        [(update, *cut)],
        [pltpu.VMEM((local, rows, COLS), BF16)] + kept_routing(groups, local, tokens, True),
        2 * local * rows * width * hidden,
        kept=(0,),
    )[0]


def base_body(w, mom, *bases):
    whole = (w[...].astype(F32) - (STEP_SIZE * MOMENTUM_DECAY) * mom[...].astype(F32)).astype(BF16)
    start = 0
    for base in bases:
        base[...] = whole[:, start : start + base.shape[1]]
        start += base.shape[1]


def base_out(proj_out, mom_out):
    local, hidden, width = proj_out.shape
    cut = ((local, hidden, COLS), lambda j: (0, 0, j))
    unit = hidden // 24
    outs = [(shape((local, n * unit, width), BF16), (local, n * unit, COLS), lambda j: (0, 0, j)) for n in PIECES]
    kept = range(len(outs))
    return kernel_call(base_body, (width // COLS,), [(proj_out, *cut), (mom_out, *cut)], outs, kept=kept)


def grad_in_body(scale, turned, grad_joint, w, mom, *rest):
    update, new_mom = rest[-2:]
    moment = MOMENTUM_DECAY * mom[0].astype(F32) + nn(turned[0], grad_joint[0]) * scale
    new_mom[0] = moment.astype(BF16)
    update[0] = (w[0].astype(F32) - STEP_SIZE * moment).astype(BF16)


def grad_in(turned_rows, grad_joint, proj_in, mom_in, start, depth, held):
    local, width, double = proj_in.shape
    rows = turned_rows.shape[2]
    first = start // DEEP
    cut = ((1, DEEP, double), lambda a, i: (a, first + i, 0))
    ins = [
        (turned_rows, (1, DEEP, rows), lambda a, i: (a, first + i, 0)),
        (grad_joint, (1, rows, double), lambda a, i: (a, 0, 0)),
        (proj_in, *cut),
        (mom_in, *cut),
    ]
    if held is not None:
        ins.append((held, None, None))
    return kernel_call(
        partial(grad_in_body, 1.0 / math.sqrt(width)),
        (local, depth // DEEP),
        ins,
        [(shape((local, depth, double), BF16), (1, DEEP, double), lambda a, i: (a, i, 0)), (proj_in, *cut)],
        flops=2 * local * rows * depth * double,
        aliases={4: 1} if held is not None else None,
        kept=(1,),
    )


def average_body(own, peer, *rest):
    rest[-1][...] = (0.5 * (own[...].astype(F32) + peer[...].astype(F32))).astype(BF16)


def average(own, peer, like, start, held):
    local, depth, double = own.shape
    block = (1, DEEP, double)
    ins = [(own, block, lambda a, i: (a, i, 0)), (peer, block, lambda a, i: (a, i, 0))]
    if held is not None:
        ins.append((held, None, None))
    return kernel_call(
        average_body,
        (local, depth // DEEP),
        ins,
        [(like, block, lambda a, i: (a, start // DEEP + i, 0))],
        aliases={2: 0} if held is not None else None,
        kept=(0,),
    )[0]


def returns_body(groups, local, scale, product, left, w, mine, own, other, rows, hot, weight=None):
    find_rows(mine, local, hot, weight)
    for a in range(local):
        rows[a] = (product(left[a], w[a]) * scale).astype(rows.dtype)
    for k in range(groups):
        parts = jnp.concatenate([rows[a, k * CAP : (k + 1) * CAP, :] for a in range(local)], axis=0)
        if weight is not None:
            parts = parts * weight[k]
        part = tn(hot[k], parts.astype(BF16))
        if k % 2 == 0:
            own[k // 2] = part
        else:
            other[k // 2] = part.astype(BF16)


def returns(left, w, mine, weighted):
    groups, _, tokens = mine.shape
    local, rows, inside = left.shape
    whole = lambda j: (0, 0, 0)
    if weighted:
        product, width, cut, scale = nn, w.shape[2], ((local, inside, COLS), lambda j: (0, 0, j)), 1.0 / math.sqrt(inside)
    else:
        product, width, cut, scale = nt, w.shape[1], ((local, COLS, inside), lambda j: (0, j, 0)), 1.0 / math.sqrt(w.shape[1])
    out = ((groups // 2, tokens, COLS), lambda j: (0, 0, j))
    return kernel_call(
        partial(returns_body, groups, local, scale, product),
        (width // COLS,),
        [(left, left.shape, whole), (w, *cut), (mine, mine.shape, whole)],
        [(shape((groups // 2, tokens, width), F32), *out), (shape((groups // 2, tokens, width), BF16), *out)],
        [pltpu.VMEM((local, rows, COLS), F32 if weighted else BF16)] + kept_routing(groups, local, tokens, weighted),
        2 * local * rows * width * inside,
    )


def columns(array):
    lead = array.shape[:-1]
    return array, (*lead, COLS) if lead else SCALARS, lambda j: (*(0 for _ in lead), j)


def line_end():
    chip = lax.axis_index("exp") // 2
    return ((chip == 0) | (chip == 3)).astype(jnp.int32)[None]


def by_columns(body, ins, outs, kept=()):
    return kernel_call(body, (outs[0].shape[-1] // COLS,), [columns(a) for a in ins], [columns(a) for a in outs], kept=kept)


def middle_body(ends, value, far, out):
    out[...] = jnp.where(ends[0] > 0, value[...], far[...])


def middle_of(value, found, ends):
    if len(found) != 2:
        return value
    return by_columns(middle_body, [ends, value, found[1]], [value])[0]


def paired_body(base, own, other, total, *parts):
    total[...] = base[...].astype(F32) + (own[0] + other[0].astype(F32))
    for s, part in enumerate(parts):
        part[...] = (own[s + 1] + other[s + 1].astype(F32)).astype(BF16)


def paired(base, own, other):
    out = by_columns(paired_body, [base, own, swap(other)], [shape(base.shape, F32)] + [base] * (own.shape[0] - 1))
    return out[0], out[1:]


def far_body(ends, part, middle, out):
    heard = jnp.where(ends[0] > 0, 0.0, middle[...].astype(F32))
    out[...] = (part[...].astype(F32) + heard).astype(BF16)


def send_last(parts, heard, ends):
    if len(parts) != 3:
        return heard
    far = by_columns(far_body, [ends, parts[2], heard[0]], [parts[2]])[0]
    return [*heard, to_xor(far, 6)]


def added_body(line, ends, total, *refs):
    out, heard = refs[-1], [ref[...].astype(F32) for ref in refs[:-1]]
    if line:
        heard[0] = jnp.where(ends[0] > 0, heard[0], 0.0)
    out[...] = sum(heard, total[...]).astype(BF16)


def added(total, heard, ends):
    line = lax.axis_size("exp") == 8
    return by_columns(partial(added_body, line), [ends, total, *heard], [shape(total.shape, BF16)], (0,))[0]


def routing(weights, chosen, places, local):
    groups = lax.axis_size("exp")
    tokens = chosen.shape[0]
    ids = jnp.arange(groups * local, dtype=jnp.int32)[:, None, None]
    hit = (chosen[None] == ids) & (places[None] < CAP)
    place_of = (jnp.sum(jnp.where(hit, places[None] + 1, 0), axis=2) - 1).astype(F32)
    weight_of = jnp.sum(jnp.where(hit, weights[None], 0.0), axis=2)
    packed = jnp.stack([place_of, weight_of], axis=1).reshape(groups, 2 * local, tokens)
    arrived = lax.all_to_all(packed, "exp", split_axis=0, concat_axis=0, tiled=True)
    return arrived[lax.axis_index("exp") ^ jnp.arange(groups, dtype=jnp.int32)]


def step(inputs, upstream, weights, chosen, places, proj_in, proj_out, mom_in, mom_out, bit):
    local, width, _ = proj_in.shape
    depth = 512

    ties = lax.optimization_barrier
    ends = line_end()
    first_rows = 3 * DEEP

    tok = near_and_far(inputs)
    peer_upstream = gossip(upstream, bit)
    mine = routing(weights, chosen, places, local)
    bases = base_out(proj_out, mom_out)
    peer_bases = [gossip(after(bases[0], peer_upstream), bit)]
    *tok, mine, peer_upstream, peer_bases[0] = ties((*tok, mine, peer_upstream, peer_bases[0]))
    sent = middle_of(inputs, tok, ends)
    tok_same = all_blocks(inputs, tok, sent)
    peer_bases.append(gossip(after(bases[1], sent), bit))
    peer_mine = gossip(after(mine, sent), bit)

    *tok_same, peer_bases[1], peer_mine = ties((*tok_same, peer_bases[1], peer_mine))
    upstream_now, base = ties((upstream, bases[2], *tok_same[1:], peer_bases[1]))[:2]
    cot = near_and_far(upstream_now)
    peer_bases.append(gossip(base, bit))
    turned_rows, inner, packet, slope, value = forward(with_other_core(tok_same), mine, proj_in, proj_out, mom_out)
    own, other = returns(inner, proj_out, mine, True)
    *cot, own, peer_bases[2] = ties((*cot, own, peer_bases[2]))
    sent = middle_of(upstream, cot, ends)
    cot_same = all_blocks(upstream, cot, sent)
    peer_bases.append(gossip(after(bases[3], sent), bit))
    total_1, parts_1 = paired(inputs, own, after(other, sent))

    early = [0, 1, 3] if len(cot_same) == 4 else []
    swapped = {s: swap(cot_same[s]) for s in early}
    *cot_same, total_1, peer_bases[3], swapped = ties((*cot_same, total_1, peer_bases[3], swapped))
    peer_packet = gossip(after(packet, peer_bases[3]), bit)
    cot_all = [part for s, block in enumerate(cot_same) for part in (block, swapped[s] if s in swapped else swap(block))]
    new_mom_out, update_out, grad_joint = backward(cot_all, mine, packet, slope, value, proj_out, mom_out)
    update_0, new_mom_in = grad_in(turned_rows, grad_joint, proj_in, mom_in, 0, first_rows, None)
    peer_0 = gossip(update_0, bit)
    new_mom_in, peer_packet = ties((new_mom_in, peer_packet))
    heard_1 = send_first(parts_1, cot_same[2])
    there = near_and_far(after(peer_upstream, cot_same[2]))
    last = width - DEEP
    update_1, new_mom_in = grad_in(turned_rows, grad_joint, proj_in, mom_in, first_rows, last - first_rows, new_mom_in)
    peer_1 = gossip(update_1, bit)
    update_2, new_mom_in = grad_in(turned_rows, grad_joint, proj_in, mom_in, last, DEEP, new_mom_in)
    peer_2 = gossip(update_2, bit)
    own, other = returns(after(grad_joint, update_2), proj_in, mine, False)

    *there, own, heard_1[0] = ties((*there, own, *heard_1))[: len(there) + 2]
    heard_1 = send_last(parts_1, heard_1, ends)
    sent = middle_of(peer_upstream, there, ends)
    there_same = all_blocks(peer_upstream, there, sent)
    total_2, parts_2 = paired(upstream, own, after(other, sent))
    new_w_in = average(update_0, after(peer_0, total_2), proj_in, 0, None)

    *there_same, new_w_in, heard_1[-1] = ties((*there_same, new_w_in, heard_1[-1]))
    layer_out = added(total_1, heard_1, ends)
    heard_2 = send_first(parts_2, there_same[2])
    there_all = with_other_core(there_same)
    new_w_out = peer_out(there_all, peer_mine, peer_packet, peer_bases, update_out)
    *heard_2, new_w_out, layer_out = ties((*heard_2, new_w_out, layer_out))
    grad_tokens = added(total_2, send_last(parts_2, heard_2, ends), ends)

    new_w_in = average(update_1, after(peer_1, grad_tokens), proj_in, first_rows, new_w_in)
    new_w_in = average(update_2, peer_2, proj_in, last, new_w_in)
    return tuple(v[None] for v in (layer_out, grad_tokens, new_w_in, new_w_out, new_mom_in, new_mom_out))


def shards(tokens, cotangent, route_weight, expert_ids, slots, gossip_round, w_in, w_out, mom_in, mom_out):
    levels = lax.axis_size("rep").bit_length() - 1
    round_now = jnp.remainder(gossip_round[0], jnp.int32(levels))
    operands = [v[0] for v in (tokens, cotangent, route_weight, expert_ids, slots, w_in, w_out, mom_in, mom_out)]
    return lax.switch(round_now, [partial(step, bit=bit) for bit in range(levels)], *operands)


def solution(mesh):
    three, four = P("rep", "exp", None), P("rep", "exp", None, None)
    return jax.shard_map(
        shards,
        mesh=mesh,
        in_specs=(three, three, three, three, three, P(), four, four, four, four),
        out_specs=(three, three, four, four, four, four),
        check_vma=False,
    )
```
